32 devices in a mesh: dp: 8 (over y, x, core), tensor: 4 (over z).
Axes of the slice: x: 2, y: 2, z: 4, core: 2. Of those that a mesh axis runs over, the one named last changes fastest.
Arguments:
- tokens: bfloat16 [4096, 1536], P(('dp', 'tensor')), may hold values from -6 to 6
- grad_out: bfloat16 [4096, 1536], P(('dp', 'tensor')), may hold values from -6 to 6
- attn_gain: float32 [1536], replicated, may hold values from 0.1 to 1.9
- w_query: bfloat16 [1536, 1536], P('dp', 'tensor'), may hold values from -0.15625 to 0.15625
- b_query: float32 [1536], replicated, may hold values from -2 to 2
- w_key: bfloat16 [1536, 256], P('dp'), may hold values from -0.15625 to 0.15625
- b_key: float32 [256], replicated, may hold values from -2 to 2
- w_value: bfloat16 [1536, 256], P('dp'), may hold values from -0.15625 to 0.15625
- b_value: float32 [256], replicated, may hold values from -1.5 to 1.5
- w_out: bfloat16 [1536, 1536], P('dp', 'tensor'), may hold values from -0.3125 to 0.3125
- mlp_gain: float32 [1536], replicated, may hold values from 0.1 to 1.9
- w_gate: bfloat16 [1536, 8960], P('dp', 'tensor'), may hold values from -0.15625 to 0.15625
- w_up: bfloat16 [1536, 8960], P('dp', 'tensor'), may hold values from -0.15625 to 0.15625
- w_down: bfloat16 [1536, 8960], P('dp', 'tensor'), may hold values from -0.125 to 0.125
Outputs:
- out: float32 [4096, 1536], P(('dp', 'tensor'))
- grad_in: float32 [4096, 1536], P(('dp', 'tensor'))
- grad_attn_gain: float32 [1536], P(('dp', 'tensor'))
- grad_w_query: float32 [1536, 1536], P('dp', 'tensor')
- grad_b_query: float32 [1536], P(('dp', 'tensor'))
- grad_w_key: float32 [1536, 256], P(('dp', 'tensor'))
- grad_b_key: float32 [256], P(('dp', 'tensor'))
- grad_w_value: float32 [1536, 256], P(('dp', 'tensor'))
- grad_b_value: float32 [256], P(('dp', 'tensor'))
- grad_w_out: float32 [1536, 1536], P('dp', 'tensor')
- grad_mlp_gain: float32 [1536], P(('dp', 'tensor'))
- grad_w_gate: float32 [1536, 8960], P('dp', 'tensor')
- grad_w_up: float32 [1536, 8960], P('dp', 'tensor')
- grad_w_down: float32 [1536, 8960], P('dp', 'tensor')
The draws below stay inside these ranges and needn't reach their ends.
All inputs are finite; a program needn't handle non-finite values.
Results may differ from the reference program's by a relative error of at most 0.04.
Values may be sent and summed in bfloat16 or wider, within the bound.
A program may use at most 192 MiB of HBM per device.

```python
import math
import jax
import jax.numpy as jnp
from jax import lax

D = 1536
HQ = 12
KVH = 2
HD = 128
FF = 8960
CLEN = 512
GROUPS = 4
GROUP_TOK = 1024
PROMPT = 512
TOKENS = 4096


def raised(values, own_key, source, target, shards_of, factor):
    owner, partner = [(jnp.arange(values.shape[axis_at]) // (values.shape[axis_at] // shards_of)).reshape([-1 if axis == axis_at else 1 for axis in range(values.ndim)]) for axis_at in (source, target)]
    chosen = jax.random.permutation(own_key, shards_of)[partner]
    strong = (owner == chosen) | (owner == (partner + shards_of // 2) % shards_of)
    return jnp.where(strong, factor * values, values)


def shard_levels(stream_key, shape, cuts, smallest, largest):
    factor_of, own = 1.0, jax.random.fold_in(stream_key, 6)
    for dim, blocks in cuts:
        draws = jnp.exp(jax.random.uniform(jax.random.fold_in(own, dim), (blocks,), jnp.float32, smallest / len(cuts), largest / len(cuts)))
        factor_of = factor_of * jnp.repeat(draws, shape[dim] // blocks).reshape([-1 if axis == dim else 1 for axis in range(len(shape))])
    return factor_of


def gaussian(stream_key, dims, scale, bound, shards=(), kind=jnp.bfloat16):
    drawn = scale * jax.random.normal(stream_key, dims, jnp.float32)
    if shards:
        drawn = drawn * shard_levels(stream_key, dims, shards, -0.22, 0.18)
    return jnp.clip(drawn, -bound, bound).astype(kind)


def heavy_noise(rng, extent, spread, most, split, heavy, kind=jnp.bfloat16):
    array = spread * jax.random.normal(rng, extent, jnp.float32)
    if split:
        array = array * shard_levels(rng, extent, split, -0.22, 0.18)
    return jnp.clip(raised(array, jax.random.fold_in(rng, 3), *heavy), -most, most).astype(kind)


def setup_inputs(seed: int = 0) -> dict:
    key_of = jax.random.split(jax.random.key(seed), 15)
    tokens = heavy_noise(key_of[0], (TOKENS, D), 1.0, 6.0, ((0, 32),), (0, 1, 32, 2.75))
    grad_out = heavy_noise(key_of[1], (TOKENS, D), 1.0, 6.0, ((0, 32),), (0, 1, 32, 2.75))
    attn_gain = jnp.clip(1.0 + 0.18 * jax.random.normal(key_of[2], (D,), jnp.float32), 0.1, 1.9)
    w_query = gaussian(key_of[3], (D, HQ * HD), D ** -0.5, 0.15625, ((0, 8), (1, 4)))
    b_query = gaussian(key_of[4], (HQ * HD,), 0.3, 2.0, (), jnp.float32)
    w_key = gaussian(key_of[5], (D, KVH * HD), D ** -0.5, 0.15625, ((0, 8),))
    b_key = gaussian(key_of[6], (KVH * HD,), 0.3, 2.0, (), jnp.float32)
    w_value = gaussian(key_of[7], (D, KVH * HD), D ** -0.5, 0.15625, ((0, 8),))
    b_value = gaussian(key_of[8], (KVH * HD,), 0.2, 1.5, (), jnp.float32)
    w_out = gaussian(key_of[9], (D, HQ * HD), (HQ * HD // 4) ** -0.5, 0.3125, ((0, 8), (1, 4)))
    mlp_gain = jnp.clip(1.0 + 0.18 * jax.random.normal(key_of[10], (D,), jnp.float32), 0.1, 1.9)
    w_gate = gaussian(key_of[11], (D, FF), D ** -0.5, 0.15625, ((0, 8), (1, 4)))
    w_up = gaussian(key_of[12], (D, FF), D ** -0.5, 0.15625, ((0, 8), (1, 4)))
    w_down = gaussian(key_of[13], (D, FF), (FF // 4) ** -0.5, 0.125, ((0, 8), (1, 4)))
    return dict(tokens=tokens, grad_out=grad_out, attn_gain=attn_gain, w_query=w_query, b_query=b_query, w_key=w_key, b_key=b_key, w_value=w_value, b_value=b_value, w_out=w_out, mlp_gain=mlp_gain, w_gate=w_gate, w_up=w_up, w_down=w_down)


EPS = 1e-06
BASE = 1000000.0
NEG = -1e+30

@jax.custom_vjp
def low(v):
    return lax.optimization_barrier(v.astype(jnp.bfloat16)).astype(jnp.float32)

@jax.custom_vjp
def low_back(v):
    return v

def low_keep(v):
    return (low(v), None)

def low_pass(kept, grad):
    return (grad,)

def back_keep(v):
    return (v, None)

def back_low(kept, grad):
    return (low(grad),)
low.defvjp(low_keep, low_pass)
low_back.defvjp(back_keep, back_low)

def normed(rows, gain):
    return rows * lax.rsqrt(lax.optimization_barrier(jnp.mean(rows * rows, -1, keepdims=True)) + EPS) * gain

def tables(position, head_dim):
    freq = BASE ** (-(jnp.arange(head_dim // 2, dtype=jnp.float32) * 2.0 / head_dim))
    angle = position.astype(jnp.float32)[:, None] * freq[None, :]
    return (jnp.concatenate([jnp.cos(angle), jnp.cos(angle)], -1), jnp.concatenate([jnp.sin(angle), jnp.sin(angle)], -1))

def rotate(values, cosine, sine):
    half = values.shape[-1] // 2
    turned = jnp.concatenate([-values[..., half:], values[..., :half]], -1)
    return values * cosine + turned * sine

def layout(count):
    local = jnp.arange(count, dtype=jnp.int32)
    later = jnp.maximum(local - PROMPT, 0)
    in_prompt = local < PROMPT
    position = jnp.where(in_prompt, local, PROMPT + later % CLEN)
    segment = jnp.where(in_prompt, 0, 1 + later // CLEN)
    return (position, segment)

def matmul(left, right):
    return jnp.dot(left, right, precision=lax.Precision.HIGHEST)

def attend(queries, keys, values, position, segment):
    width = min(512, GROUP_TOK)
    share = HQ // KVH

    def one_block(inputs):
        block_queries, block_position, block_segment = inputs
        grouped = block_queries.reshape(width, KVH, share, HD)
        raw = jnp.einsum('qgsd,kgd->gsqk', grouped, keys, precision=lax.Precision.HIGHEST)
        scores = low_back(raw * (1.0 / math.sqrt(HD)))
        allowed = (position[None, :] <= block_position[:, None]) & ((segment[None, :] == 0) | (segment[None, :] == block_segment[:, None]))
        scores = jnp.where(allowed[None, None], scores, NEG)
        peak = lax.optimization_barrier(jnp.max(scores, -1, keepdims=True))
        weights = jnp.exp(scores - peak)
        probs = low(weights / lax.optimization_barrier(jnp.sum(weights, -1, keepdims=True)))
        mixed = jnp.einsum('gsqk,kgd->qgsd', probs, values, precision=lax.Precision.HIGHEST)
        return mixed.reshape(width, HQ * HD)
    blocks = (queries.reshape(GROUP_TOK // width, width, HQ, HD), position.reshape(GROUP_TOK // width, width), segment.reshape(GROUP_TOK // width, width))
    return lax.map(jax.checkpoint(one_block), blocks).reshape(GROUP_TOK, HQ * HD)

def group_layer(params, rows):
    attn_gain, w_query, b_query, w_key, b_key, w_value, b_value, w_out, mlp_gain, w_gate, w_up, w_down = params
    position, segment = layout(GROUP_TOK)
    cosine, sine = tables(position, HD)
    normal_in = low(normed(rows, attn_gain))
    query_lin = low_back(matmul(normal_in, w_query) + b_query).reshape(GROUP_TOK, HQ, HD)
    key_lin = low_back(matmul(normal_in, w_key) + b_key).reshape(GROUP_TOK, KVH, HD)
    value_lin = low_back(matmul(normal_in, w_value) + b_value).reshape(GROUP_TOK, KVH, HD)
    queries = low(rotate(query_lin, cosine[:, None], sine[:, None]))
    keys = low(rotate(key_lin, cosine[:, None], sine[:, None]))
    values = low(value_lin)
    mixed = low(low_back(attend(queries, keys, values, position, segment)))
    branch = low_back(matmul(mixed, w_out.T))
    middle = rows + branch
    normal_mid = low(normed(middle, mlp_gain))
    gate = low_back(matmul(normal_mid, w_gate))
    up = low_back(matmul(normal_mid, w_up))
    hidden = low(jax.nn.silu(gate) * up)
    return middle + matmul(hidden, w_down.T)

def forward(params, inputs):

    def one_group(carry, rows):
        return (carry, jax.checkpoint(group_layer)(params, rows))
    carry, outputs = lax.scan(one_group, jnp.zeros((), jnp.float32), inputs.reshape(GROUPS, GROUP_TOK, D))
    return outputs.reshape(TOKENS, D)

def reference(tokens, grad_out, attn_gain, w_query, b_query, w_key, b_key, w_value, b_value, w_out, mlp_gain, w_gate, w_up, w_down):
    params = tuple((item.astype(jnp.float32) for item in (attn_gain, w_query, b_query, w_key, b_key, w_value, b_value, w_out, mlp_gain, w_gate, w_up, w_down)))
    outputs, pull = jax.vjp(forward, params, tokens.astype(jnp.float32))
    grads, grad_in = pull(grad_out.astype(jnp.float32))
    return (outputs, grad_in, grads[0], grads[1], grads[2], grads[3], grads[4], grads[5], grads[6], grads[7], grads[8], grads[9], grads[10], grads[11])
```

```python
import functools
from functools import reduce
import math

import jax
import jax.numpy as jnp
from jax import lax
from jax.experimental import pallas as pl
from jax.experimental.pallas import tpu as pltpu
from jax.sharding import PartitionSpec as P

HD = 128
CLEN = 512
GROUPS = 4


EPS = 1e-06
BASE = 1000000.0
NEG = -1e30


def from_behind(x, axis, by):
    size = lax.axis_size(axis)
    pairs = [(i, i + by) for i in range(size) if 0 <= i + by < size]
    return lax.ppermute(x, axis, pairs)


def swapped(value, axis, apart):
    mask = 2**apart
    pairs = [(source, source ^ mask) for source in range(lax.axis_size(axis))]
    return lax.ppermute(value, axis, pairs)


def normed(rows, gain):
    return rows * lax.rsqrt(jnp.mean(rows * rows, -1, keepdims=True) + EPS) * gain


def tables(position, head_dim):
    freq = BASE ** (-(jnp.arange(head_dim // 2, dtype=jnp.float32) * 2.0 / head_dim))
    angle = position.astype(jnp.float32)[:, None] * freq[None, :]
    return (
        jnp.concatenate([jnp.cos(angle), jnp.cos(angle)], -1),
        jnp.concatenate([jnp.sin(angle), jnp.sin(angle)], -1),
    )


def rotate(values, cosine, sine):
    half = values.shape[-1] // 2
    turned = jnp.concatenate([-values[..., half:], values[..., :half]], -1)
    return values * cosine + turned * sine


def layout(start, count, group_tok, prompt):
    index = start + jnp.arange(count, dtype=jnp.int32)
    local = index % group_tok
    later = jnp.maximum(local - prompt, 0)
    in_prompt = local < prompt
    position = jnp.where(in_prompt, local, prompt + later % CLEN)
    segment = jnp.where(in_prompt, 0, 1 + later // CLEN)
    return (position, segment)


def activation(gate_in, up_in):
    return jax.nn.silu(gate_in) * up_in


def block_scores(queries, keys_block, allowed):
    scores = jnp.einsum("hqd,kd->hqk", queries, keys_block, preferred_element_type=jnp.float32) * (
        1.0 / math.sqrt(HD)
    )
    if allowed is None:
        return scores
    return jnp.where(allowed[None], scores, NEG)


def block_peak(queries, keys_block, allowed):
    scores = block_scores(queries, keys_block, allowed)
    peak = jnp.max(scores, -1)
    return (peak, jnp.sum(jnp.exp(scores - peak[..., None]), -1))


def block_mix(queries, keys_block, values_block, allowed, spread):
    probs = jnp.exp(block_scores(queries, keys_block, allowed) - spread[..., None]).astype(
        jnp.bfloat16
    )
    return jnp.einsum("hqk,kd->hqd", probs, values_block, preferred_element_type=jnp.float32)


def block_back(queries, keys_block, values_block, allowed, spread, d_mixed, offset_terms):
    probs = jnp.exp(block_scores(queries, keys_block, allowed) - spread[..., None])
    d_values = jnp.einsum(
        "hqk,hqd->kd", probs.astype(jnp.bfloat16), d_mixed, preferred_element_type=jnp.float32
    )
    d_probs = jnp.einsum("hqd,kd->hqk", d_mixed, values_block, preferred_element_type=jnp.float32)
    d_scores = (probs * (d_probs - offset_terms[..., None])).astype(jnp.bfloat16)
    scale = 1.0 / math.sqrt(HD)
    d_queries = (
        jnp.einsum("hqk,kd->hqd", d_scores, keys_block, preferred_element_type=jnp.float32) * scale
    )
    d_keys = (
        jnp.einsum("hqk,hqd->kd", d_scores, queries, preferred_element_type=jnp.float32) * scale
    )
    return (d_queries, jnp.concatenate([d_keys, d_values], 1))


def reduce_weights(terms):
    return (
        lax.psum_scatter(
            terms[0].astype(jnp.bfloat16), "dp", scatter_dimension=0, tiled=True
        ).astype(jnp.float32),
        lax.psum_scatter(
            terms[1].astype(jnp.bfloat16), "dp", scatter_dimension=0, tiled=True
        ).astype(jnp.float32),
        lax.psum_scatter(
            terms[2].astype(jnp.bfloat16), "dp", scatter_dimension=0, tiled=True
        ).astype(jnp.float32),
        lax.psum_scatter(
            terms[3].astype(jnp.bfloat16), "dp", scatter_dimension=0, tiled=True
        ).astype(jnp.float32),
        lax.psum_scatter(
            terms[4].astype(jnp.bfloat16), "dp", scatter_dimension=0, tiled=True
        ).astype(jnp.float32),
    )


def shards(
    tokens,
    grad_out,
    attn_gain,
    w_query,
    b_query,
    w_key,
    b_key,
    w_value,
    b_value,
    w_out,
    mlp_gain,
    w_gate,
    w_up,
    w_down,
):
    tensor_count = lax.axis_size("tensor")
    data_count = lax.axis_size("dp")
    tensor_index = lax.axis_index("tensor")
    data_index = lax.axis_index("dp")
    rows = tokens.shape[0] * tensor_count
    members = data_count // GROUPS
    group_tok = members * rows
    prompt = group_tok // 2
    offset = data_index % members
    query_width = w_query.shape[1]
    heads = query_width // HD
    key_width = w_key.shape[1]
    key_head = tensor_index // (tensor_count // (key_width // HD))
    width_model = tokens.shape[1]
    inputs = tokens.astype(jnp.float32)
    normal_in = normed(inputs, attn_gain)
    rows_in, rows_grad = (
        lax.all_gather(normal_in.astype(jnp.bfloat16), "tensor", axis=0, tiled=True),
        lax.all_gather(grad_out, "tensor", axis=0, tiled=True),
    )
    key_cols = lax.dynamic_slice_in_dim(w_key, key_head * HD, HD, 1)
    value_cols = lax.dynamic_slice_in_dim(w_value, key_head * HD, HD, 1)
    pair_cols = jnp.concatenate([key_cols, value_cols], 1)
    full_query, full_pair, full_out, full_gate, full_up, full_down = (
        lax.all_gather(w_query, "dp", axis=0, tiled=True),
        lax.all_gather(pair_cols, "dp", axis=0, tiled=True),
        lax.all_gather(w_out, "dp", axis=0, tiled=True),
        lax.all_gather(w_gate, "dp", axis=0, tiled=True),
        lax.all_gather(w_up, "dp", axis=0, tiled=True),
        lax.all_gather(w_down, "dp", axis=0, tiled=True),
    )
    query_bias = lax.dynamic_slice_in_dim(b_query, tensor_index * query_width, query_width, 0)
    pair_bias = jnp.concatenate(
        [
            lax.dynamic_slice_in_dim(b_key, key_head * HD, HD, 0),
            lax.dynamic_slice_in_dim(b_value, key_head * HD, HD, 0),
        ]
    )
    query_lin = jnp.dot(rows_in, full_query, preferred_element_type=jnp.float32) + query_bias
    pair_lin = jnp.dot(rows_in, full_pair, preferred_element_type=jnp.float32) + pair_bias
    position, segment = layout(data_index * rows, rows, group_tok, prompt)
    cosine, sine = tables(position, HD)

    def turned(values):
        return rotate(values, cosine, sine)

    query_heads = query_lin.reshape(rows, heads, HD).transpose(1, 0, 2)
    key_lin = pair_lin[:, :HD]
    queries = turned(query_heads).astype(jnp.bfloat16)
    keys = turned(key_lin).astype(jnp.bfloat16)
    values = pair_lin[:, HD:].astype(jnp.bfloat16)
    allowed = (position[None, :] <= position[:, None]) & (
        (segment[None, :] == 0) | (segment[None, :] == segment[:, None])
    )
    remote = []
    for step in range(1, members):
        keys_far, values_far = from_behind((keys, values), "dp", step)
        usable = (offset >= step) & (offset - step < members // 2)
        remote.append((keys_far, values_far, usable))
    empty_peak = jnp.full((heads, rows), NEG, jnp.float32)
    empty_total = jnp.zeros((heads, rows), jnp.float32)
    empty_mix = jnp.zeros((heads, rows, HD), jnp.float32)

    def far_peak(keys_block):
        return block_peak(queries, keys_block, None)

    def skip_peak(keys_block):
        return (empty_peak, empty_total)

    peaks = [block_peak(queries, keys, allowed)]
    for keys_far, values_far, usable in remote:
        peaks.append(lax.cond(usable, far_peak, skip_peak, keys_far))
    peak = reduce(jnp.maximum, [entry[0] for entry in peaks])
    total = reduce(jnp.add, [entry[1] * jnp.exp(entry[0] - peak) for entry in peaks])
    spread = peak + jnp.log(total)

    def far_mix(keys_block, values_block):
        return block_mix(queries, keys_block, values_block, None, spread)

    def skip_mix(keys_block, values_block):
        return empty_mix

    mixed = block_mix(queries, keys, values, allowed, spread)
    for keys_far, values_far, usable in remote:
        mixed = mixed + lax.cond(usable, far_mix, skip_mix, keys_far, values_far)
    mixed_rows = mixed.transpose(1, 0, 2).reshape(rows, query_width).astype(jnp.bfloat16)
    branch = jnp.einsum("rq,dq->rd", mixed_rows, full_out, preferred_element_type=jnp.float32)
    middle = inputs + lax.psum_scatter(
        branch.astype(jnp.bfloat16), "tensor", scatter_dimension=0, tiled=True
    ).astype(jnp.float32)
    normal_mid = normed(middle, mlp_gain)
    rows_mid = lax.all_gather(normal_mid.astype(jnp.bfloat16), "tensor", axis=0, tiled=True)
    gate = jnp.dot(rows_mid, full_gate, preferred_element_type=jnp.float32)
    up = jnp.dot(rows_mid, full_up, preferred_element_type=jnp.float32)
    hidden = activation(gate, up).astype(jnp.bfloat16)
    down_part = jnp.einsum("rf,df->rd", hidden, full_down, preferred_element_type=jnp.float32)
    result = middle + lax.psum_scatter(
        down_part.astype(jnp.bfloat16), "tensor", scatter_dimension=0, tiled=True
    ).astype(jnp.float32)
    back_query, back_pair, back_out, back_gate, back_up, back_down = (
        lax.all_gather(w_query, "dp", axis=0, tiled=True),
        lax.all_gather(pair_cols, "dp", axis=0, tiled=True),
        lax.all_gather(w_out, "dp", axis=0, tiled=True),
        lax.all_gather(w_gate, "dp", axis=0, tiled=True),
        lax.all_gather(w_up, "dp", axis=0, tiled=True),
        lax.all_gather(w_down, "dp", axis=0, tiled=True),
    )
    d_hidden = jnp.dot(rows_grad, back_down, preferred_element_type=jnp.float32)
    grad_down = jnp.einsum("rd,rf->df", rows_grad, hidden, preferred_element_type=jnp.float32)
    d_gate, d_up = jax.vjp(activation, gate, up)[1](d_hidden)
    d_gate = d_gate.astype(jnp.bfloat16)
    d_up = d_up.astype(jnp.bfloat16)
    grad_gate = jnp.einsum("rd,rf->df", rows_mid, d_gate, preferred_element_type=jnp.float32)
    grad_up = jnp.einsum("rd,rf->df", rows_mid, d_up, preferred_element_type=jnp.float32)
    d_mid_rows = jnp.einsum(
        "rf,df->rd", d_gate, back_gate, preferred_element_type=jnp.float32
    ) + jnp.einsum("rf,df->rd", d_up, back_up, preferred_element_type=jnp.float32)
    d_mid = lax.psum_scatter(
        d_mid_rows.astype(jnp.bfloat16), "tensor", scatter_dimension=0, tiled=True
    ).astype(jnp.float32)
    d_middle_norm, grad_mlp_gain = jax.vjp(normed, middle, mlp_gain)[1](d_mid)
    d_middle = grad_out.astype(jnp.float32) + d_middle_norm
    rows_back = lax.all_gather(d_middle.astype(jnp.bfloat16), "tensor", axis=0, tiled=True)
    grad_proj = jnp.einsum("rd,rq->dq", rows_back, mixed_rows, preferred_element_type=jnp.float32)
    d_mixed_rows = jnp.dot(rows_back, back_out, preferred_element_type=jnp.float32).astype(
        jnp.bfloat16
    )
    d_mixed = d_mixed_rows.reshape(rows, heads, HD).transpose(1, 0, 2)
    offset_terms = jnp.sum(d_mixed.astype(jnp.float32) * mixed, -1)

    def far_back(keys_block, values_block):
        return block_back(queries, keys_block, values_block, None, spread, d_mixed, offset_terms)

    def skip_back(keys_block, values_block):
        return (empty_mix, jnp.zeros((rows, 2 * HD), jnp.float32))

    d_queries, d_pair = block_back(queries, keys, values, allowed, spread, d_mixed, offset_terms)
    for step, entry in enumerate(remote, 1):
        part_queries, part_pair = lax.cond(entry[2], far_back, skip_back, entry[0], entry[1])
        d_queries = d_queries + part_queries
        d_pair = d_pair + from_behind(part_pair.astype(jnp.bfloat16), "dp", -step).astype(
            part_pair.dtype
        )
    d_pair = d_pair + swapped(d_pair.astype(jnp.bfloat16), "tensor", 0).astype(d_pair.dtype)
    d_key = jax.vjp(turned, key_lin)[1](d_pair[:, :HD])[0]
    pair_low = jnp.concatenate([d_key, d_pair[:, HD:]], 1).astype(jnp.bfloat16)
    d_query_heads = jax.vjp(turned, query_heads)[1](d_queries)[0]
    d_query = d_query_heads.transpose(1, 0, 2).reshape(rows, query_width).astype(jnp.bfloat16)
    which = tensor_index % 2
    mine = lax.dynamic_slice_in_dim(pair_low, which * HD, HD, 1)
    mine_weight = lax.dynamic_slice_in_dim(back_pair, which * HD, HD, 1)
    grad_query = jnp.einsum("rd,rq->dq", rows_in, d_query, preferred_element_type=jnp.float32)
    grad_mine = jnp.einsum("rd,rk->dk", rows_in, mine, preferred_element_type=jnp.float32)
    d_in_rows = jnp.einsum(
        "rq,dq->rd", d_query, back_query, preferred_element_type=jnp.float32
    ) + jnp.einsum("rk,dk->rd", mine, mine_weight, preferred_element_type=jnp.float32)
    d_in = lax.psum_scatter(
        d_in_rows.astype(jnp.bfloat16), "tensor", scatter_dimension=0, tiled=True
    ).astype(jnp.float32)
    d_in_norm, grad_attn_gain = jax.vjp(normed, inputs, attn_gain)[1](d_in)
    grad_in = d_middle + d_in_norm
    column = which * key_width + key_head * HD
    pair_grad = lax.dynamic_update_slice(
        jnp.zeros((width_model, 2 * key_width), jnp.float32), grad_mine, (0, column)
    )
    bias_grad = lax.dynamic_update_slice(
        jnp.zeros((2 * key_width,), jnp.float32), jnp.sum(mine.astype(jnp.float32), 0), (column,)
    )
    query_bias_grad = lax.dynamic_update_slice(
        jnp.zeros((b_query.shape[0],), jnp.float32),
        jnp.sum(d_query.astype(jnp.float32), 0),
        (tensor_index * query_width,),
    )
    shared = (
        lax.psum_scatter(
            pair_grad[:, :key_width], ("dp", "tensor"), scatter_dimension=0, tiled=True
        ),
        lax.psum_scatter(
            pair_grad[:, key_width:], ("dp", "tensor"), scatter_dimension=0, tiled=True
        ),
        lax.psum_scatter(query_bias_grad, ("dp", "tensor"), scatter_dimension=0, tiled=True),
        lax.psum_scatter(bias_grad[:key_width], ("dp", "tensor"), scatter_dimension=0, tiled=True),
        lax.psum_scatter(bias_grad[key_width:], ("dp", "tensor"), scatter_dimension=0, tiled=True),
        lax.psum_scatter(grad_attn_gain, ("dp", "tensor"), scatter_dimension=0, tiled=True),
        lax.psum_scatter(grad_mlp_gain, ("dp", "tensor"), scatter_dimension=0, tiled=True),
    )
    part_query, part_proj, part_gate, part_up, part_down = reduce_weights(
        (grad_query, grad_proj, grad_gate, grad_up, grad_down)
    )
    return (
        result,
        grad_in,
        shared[5],
        part_query,
        shared[2],
        shared[0],
        shared[3],
        shared[1],
        shared[4],
        part_proj,
        shared[6],
        part_gate,
        part_up,
        part_down,
    )


F32 = jnp.float32
BF16 = jnp.bfloat16
MESH = pl.DeviceIdType.MESH
NCH = 2
HALF = 1152


def dot(a, b, ca=1, cb=0):
    return lax.dot_general(a, b, (((ca,), (cb,)), ((), ())), preferred_element_type=F32)


def rcopy(src, dst, send, recv, dev):
    return pltpu.make_async_remote_copy(
        src_ref=src, dst_ref=dst, send_sem=send, recv_sem=recv, device_id=dev, device_id_type=MESH
    )


class Place:
    def __init__(self, depth):
        self.depth = depth
        self.dp = lax.axis_index("dp")
        self.z = lax.axis_index("tensor")
        self.core = lax.rem(self.dp, 2)
        self.chip = self.dp // 2
        x, y = lax.rem(self.chip, 2), self.chip // 2
        self.xchip = self.chip + 1 - 2 * x
        self.ychip = self.chip + 2 - 4 * y
        self.dchip = 3 - self.chip
        self.sib = (self.chip * 2 + 1 - self.core, self.z)
        self.xnbr = (self.xchip * 2 + self.core, self.z)
        self.ynbr = (self.ychip * 2 + self.core, self.z)
        self.up = (self.dp, self.z + 1)
        self.down = (self.dp, self.z - 1)
        self.has_up = self.z < depth - 1
        self.has_down = self.z > 0

    def greet(self, across):
        barrier = pltpu.get_barrier_semaphore()
        others = [self.sib, self.xnbr, self.ynbr]
        if across:
            other = 1 - self.core
            others += [(self.xchip * 2 + other, self.z), (self.ychip * 2 + other, self.z)]
        for dev in others:
            pl.semaphore_signal(barrier, inc=1, device_id=dev, device_id_type=MESH)

        @pl.when(self.has_up)
        def _():
            pl.semaphore_signal(barrier, inc=1, device_id=self.up, device_id_type=MESH)

        @pl.when(self.has_down)
        def _():
            pl.semaphore_signal(barrier, inc=1, device_id=self.down, device_id_type=MESH)

        count = len(others) + self.has_up.astype(jnp.int32) + self.has_down.astype(jnp.int32)
        pl.semaphore_wait(barrier, count)


class LineGather:
    def __init__(self, place, at, send, recv):
        self.p, self.at, self.send, self.recv = place, at, send, recv

    def _copy(self, way, ch, d, s):
        dev = self.p.up if way == 0 else self.p.down
        block = self.at(ch, s)
        return rcopy(block, block, self.send.at[way, ch, d], self.recv.at[way, ch, d + 1], dev)

    def own(self, ch):
        for way, there in ((0, self.p.has_up), (1, self.p.has_down)):

            @pl.when(there)
            def _(way=way):
                self._copy(way, ch, 0, self.p.z).start()

    def step(self, ch, d):
        p = self.p
        for way in (0, 1):
            s = p.z - d if way == 0 else p.z + d
            valid = s >= 0 if way == 0 else s < p.depth
            onward = p.has_up if way == 0 else p.has_down

            @pl.when(valid)
            def _(way=way, s=s, onward=onward):
                block = self.at(ch, s)
                rcopy(
                    block, block, self.send.at[way, ch, d - 1], self.recv.at[way, ch, d], p.up
                ).wait_recv()
                if d < p.depth - 1:

                    @pl.when(onward)
                    def _():
                        self._copy(way, ch, d, s).start()

    def drain(self):
        p = self.p
        for ch in range(NCH):
            for d in range(p.depth - 1):
                for way in (0, 1):
                    s = p.z - d if way == 0 else p.z + d
                    valid = (s >= 0) & p.has_up if way == 0 else (s < p.depth) & p.has_down

                    @pl.when(valid)
                    def _(way=way, ch=ch, d=d, s=s):
                        self._copy(way, ch, d, s).wait_send()


class LineScatter:
    def __init__(self, place, part, land, send, recv):
        self.p, self.part, self.land, self.send, self.recv = place, part, land, send, recv

    def _copy(self, way, ch, d, s):
        dev = self.p.up if way == 0 else self.p.down
        return rcopy(
            self.part(ch, s),
            self.land.at[way, ch, d - 1],
            self.send.at[way, ch, d],
            self.recv.at[way, ch, d - 1],
            dev,
        )

    def _arrive(self, way, ch, d):
        here = self.land.at[way, ch, d]
        rcopy(here, here, self.send.at[way, ch, d], self.recv.at[way, ch, d], self.p.up).wait_recv()

    def step(self, ch, d):
        p = self.p
        for way in (0, 1):
            s = p.z + d if way == 0 else p.z - d
            valid = s < p.depth if way == 0 else s >= 0
            fed = p.has_down if way == 0 else p.has_up

            @pl.when(valid)
            def _(way=way, s=s, fed=fed):
                if d < p.depth - 1:

                    @pl.when(fed)
                    def _():
                        self._arrive(way, ch, d)
                        block = self.part(ch, s)
                        block[...] = (
                            block[...].astype(F32) + self.land[way, ch, d].astype(F32)
                        ).astype(BF16)

                self._copy(way, ch, d, s).start()

    def total(self, ch, out):
        p = self.p
        out[...] = self.part(ch, p.z)[...].astype(F32)
        for way, fed in ((0, p.has_down), (1, p.has_up)):

            @pl.when(fed)
            def _(way=way):
                self._arrive(way, ch, 0)
                out[...] += self.land[way, ch, 0].astype(F32)

    def drain(self):
        p = self.p
        for ch in range(NCH):
            for d in range(1, p.depth):
                for way in (0, 1):
                    s = p.z + d if way == 0 else p.z - d
                    valid = s < p.depth if way == 0 else s >= 0

                    @pl.when(valid)
                    def _(way=way, ch=ch, d=d, s=s):
                        self._copy(way, ch, d, s).wait_send()


def inverse_root(rows):
    return lax.rsqrt(jnp.mean(rows * rows, -1, keepdims=True) + EPS)


def turn(u, cosine, sine_signed):
    return u * cosine + pltpu.roll(u, HD // 2, 1) * sine_signed


def forward_kernel(
    tokens, grad_out, attn_gain, mlp_gain, w_query, w_key, w_value, w_out, w_gate, w_up, w_down,
    b_query, b_key, b_value, cosine, sine,
    big, proj, rows_in, heads_q, pair, mixed, middle, rows_mid, rows_grad,
    pad, v_proj, v_in, v_pair, v_mixed, v_mid, v_grad, part, land, total,
    big_send, big_recv, proj_send, proj_recv, own_sem, z_send, z_recv, s_send, s_recv, core_send, core_recv, out_sem,
):
    p = Place(4)
    z, core = p.z, p.core
    unit = tokens.shape[0] // NCH
    wide = unit * p.depth
    shard = w_query.shape[0]
    q_width = w_query.shape[1]

    def rows_of(ref, ch, s):
        return ref.at[pl.ds(pl.multiple_of(ch * wide + s * unit, unit), unit), :]

    gather_in = LineGather(p, lambda ch, s: rows_of(v_in, ch, s), z_send.at[0], z_recv.at[0])
    gather_grad = LineGather(
        p, lambda ch, s: rows_of(v_grad.at[core], ch, s), z_send.at[1], z_recv.at[1]
    )
    gather_mid = LineGather(
        p, lambda ch, s: rows_of(v_mid.at[core], ch, s), z_send.at[2], z_recv.at[2]
    )
    scatter = LineScatter(p, lambda ch, s: rows_of(part, ch, s), land, s_send, s_recv)

    p.greet(True)

    for ch in range(NCH):
        x = tokens[ch * unit : (ch + 1) * unit, :].astype(F32)
        a1 = (x * inverse_root(x) * attn_gain[...]).astype(BF16)
        v_in[pl.ds(pl.multiple_of(ch * wide + z * unit, unit), unit), :] = a1
        gather_in.own(ch)

    kv = pl.ds(pl.multiple_of((z // 2) * HD, HD), HD)
    mine = pl.ds(pl.multiple_of(p.dp * shard, 16), shard)
    v_proj[mine, 0:q_width] = w_query[...]
    v_proj[mine, q_width : q_width + HD] = w_key[:, kv]
    v_proj[mine, q_width + HD : q_width + 2 * HD] = w_value[:, kv]
    v_proj[mine, q_width + 2 * HD :] = w_out[...]

    def proj_rows(dp, first=0, count=shard):
        return v_proj.at[pl.ds(pl.multiple_of(dp * shard + first, 16), count), :]

    def proj_copy(k, src, dev, first=0, count=shard):
        block = proj_rows(src, first, count)
        return rcopy(block, block, proj_send.at[k], proj_recv.at[k], dev)

    half_rows = shard // 2
    d_dp = p.dchip * 2 + core
    proj_out = [
        proj_copy(0, p.dp, p.xnbr),
        proj_copy(1, p.dp, p.ynbr),
        proj_copy(2, p.dp, p.sib),
        proj_copy(3, p.ynbr[0], p.xnbr, 0, half_rows),
        proj_copy(4, p.xnbr[0], p.ynbr, half_rows, half_rows),
        proj_copy(5, p.xnbr[0], p.sib),
        proj_copy(6, p.ynbr[0], p.sib),
        proj_copy(7, d_dp, p.sib),
    ]
    other = 1 - 2 * core
    proj_in = [
        proj_copy(0, p.xnbr[0], p.xnbr),
        proj_copy(1, p.ynbr[0], p.ynbr),
        proj_copy(2, p.dp + other, p.sib),
        proj_copy(3, d_dp, p.xnbr, 0, half_rows),
        proj_copy(4, d_dp, p.ynbr, half_rows, half_rows),
        proj_copy(5, p.xnbr[0] + other, p.sib),
        proj_copy(6, p.ynbr[0] + other, p.sib),
        proj_copy(7, d_dp + other, p.sib),
    ]
    for k in range(3):
        proj_out[k].start()

    tail = w_gate.shape[1] - HALF
    whole = tail // 128 * 128
    mats = (w_gate, w_up, w_down)
    for k, mat in enumerate(mats):
        pad[k, :, 0:whole] = mat[:, HALF : HALF + whole]
        pad[k, :, whole:] = jnp.concatenate(
            [mat[:, HALF + whole :], jnp.zeros((shard, HALF - tail), BF16)], 1
        )

    def big_rows(k, dp):
        return big.at[k, pl.ds(pl.multiple_of(dp * shard, 16), shard), :]

    def half_of(k, c):
        return mats[k].at[:, 0:HALF] if c == 0 else pad.at[k]

    def big_out(k):
        copies = []
        for c in (0, 1):
            for way, chip in ((0, p.xchip), (1, p.ychip)):
                copies.append(
                    rcopy(
                        half_of(k, c),
                        big_rows(k, p.dp),
                        big_send.at[k, way, c],
                        big_recv.at[k, way, core],
                        (chip * 2 + c, z),
                    )
                )
        return copies

    def big_near(k, c):
        return rcopy(
            half_of(k, c), big_rows(k, p.dp), big_send.at[k, 2, 0], big_recv.at[k, 2, 0], p.sib
        )

    def big_keep(k, c):
        return pltpu.make_async_copy(half_of(k, c), big_rows(k, p.dp), own_sem.at[k])

    def big_in(k, way, c):
        dp = (p.xchip if way == 0 else p.ychip) * 2 + c
        block = big_rows(k, dp)
        return rcopy(block, block, big_send.at[k, way, c], big_recv.at[k, way, c], p.sib)

    def big_relay(k):
        one, two = big_rows(k, p.ychip * 2), big_rows(k, p.xchip * 2 + 1)
        return (
            rcopy(one, one, big_send.at[k, 3, 0], big_recv.at[k, 3, 0], p.xnbr),
            rcopy(two, two, big_send.at[k, 3, 1], big_recv.at[k, 3, 1], p.ynbr),
        )

    def big_start(k):
        for copy in big_out(k):
            copy.start()
        for c in (0, 1):

            @pl.when(core == 1 - c)
            def _(c=c):
                big_near(k, c).start()

            @pl.when(core == c)
            def _(c=c):
                big_keep(k, c).start()

    def big_forward(k):
        big_in(k, 1, 0).wait_recv()
        big_in(k, 0, 1).wait_recv()
        for copy in big_relay(k):
            copy.start()

    def big_finish(k):
        big_in(k, 0, 0).wait_recv()
        big_in(k, 1, 1).wait_recv()
        for i, dp in ((0, p.dchip * 2), (1, p.dchip * 2 + 1)):
            block = big_rows(k, dp)
            rcopy(block, block, big_send.at[k, 3, i], big_recv.at[k, 3, i], p.sib).wait_recv()
        block = big_rows(k, p.sib[0])
        rcopy(block, block, big_send.at[k, 2, 0], big_recv.at[k, 2, 0], p.sib).wait_recv()
        for copy in big_out(k) + list(big_relay(k)):
            copy.wait_send()
        for c in (0, 1):

            @pl.when(core == 1 - c)
            def _(c=c):
                big_near(k, c).wait_send()

            @pl.when(core == c)
            def _(c=c):
                big_keep(k, c).wait()

    big_start(0)
    for ch in range(NCH):
        gather_in.step(ch, 1)
    for ch in range(NCH):
        gather_in.step(ch, 2)
    big_start(1)
    proj_in[0].wait_recv()
    proj_out[4].start()
    proj_out[5].start()
    proj_in[1].wait_recv()
    proj_out[3].start()
    proj_out[6].start()
    for ch in range(NCH):
        rows = pl.ds(pl.multiple_of(ch * wide + z * unit, unit), unit)
        v_grad[core, rows, :] = grad_out[ch * unit : (ch + 1) * unit, :]
    for ch in range(NCH):
        gather_in.step(ch, 3)
    for ch in range(NCH):
        gather_grad.own(ch)
    for k in (3, 4):
        proj_in[k].wait_recv()
    proj_out[7].start()
    for k in (2, 5, 6, 7):
        proj_in[k].wait_recv()

    bias_q = b_query[:, pl.ds(pl.multiple_of(z * q_width, HD), q_width)]
    bias_k, bias_v = b_key[:, kv], b_value[:, kv]
    heads = q_width // HD
    for ch in range(NCH):
        rows = slice(ch * wide, (ch + 1) * wide)
        lin = dot(v_in[rows, :], v_proj[:, 0 : q_width + 2 * HD])
        c, s = cosine[rows, :], sine[rows, :]
        for h in range(heads):
            u = lin[:, h * HD : (h + 1) * HD] + bias_q[:, h * HD : (h + 1) * HD]
            heads_q[h, rows, :] = turn(u, c, s).astype(BF16)
        v_pair[core, rows, 0:HD] = turn(
            lin[:, q_width : q_width + HD] + bias_k, c, s
        ).astype(BF16)
        v_pair[core, rows, HD:] = (lin[:, q_width + HD :] + bias_v).astype(BF16)
    pair_out = rcopy(v_pair.at[core], v_pair.at[core], core_send.at[0], core_recv.at[0], p.sib)
    pair_out.start()
    pair_in = rcopy(
        v_pair.at[1 - core], v_pair.at[1 - core], core_send.at[0], core_recv.at[0], p.sib
    )
    pair_in.wait_recv()

    for ch in range(NCH):

        def one_head(h, _):
            keep = allowed(core, ch, unit, p.depth, wide)
            _, pb = softmax(heads_q[h, ch * wide : (ch + 1) * wide, :], v_pair, keep)
            o = dot(pb, both(v_pair, HD))
            v_mixed[ch * wide : (ch + 1) * wide, pl.ds(pl.multiple_of(h * HD, HD), HD)] = o.astype(
                BF16
            )
            return 0

        lax.fori_loop(0, heads, one_head, 0)
        rows = slice(ch * wide, (ch + 1) * wide)
        part[rows, :] = dot(v_mixed[rows, :], v_proj[:, q_width + 2 * HD :], 1, 1).astype(BF16)
        scatter.step(ch, 3)
    big_forward(0)
    big_start(2)
    for ch in range(NCH):
        gather_grad.step(ch, 1)
    for ch in range(NCH):
        scatter.step(ch, 2)
        scatter.step(ch, 1)
        scatter.total(ch, total)
        half = slice(ch * unit, (ch + 1) * unit)
        mid = tokens[half, :].astype(F32) + total[...]
        middle[half, :] = mid
        v_mid[core, pl.ds(pl.multiple_of(ch * wide + z * unit, unit), unit), :] = (
            mid * inverse_root(mid) * mlp_gain[...]
        ).astype(BF16)
        gather_mid.own(ch)
        if ch == 0:
            for c in range(NCH):
                gather_grad.step(c, 2)
    big_forward(1)
    for ch in range(NCH):
        gather_mid.step(ch, 1)
    for ch in range(NCH):
        gather_grad.step(ch, 3)
    for ch in range(NCH):
        gather_mid.step(ch, 2)

    def near(k, ref, ch, slot):
        block = ref.at[slot, pl.ds(ch * wide, wide), :]
        return rcopy(block, block, core_send.at[k], core_recv.at[k], p.sib)

    for ch in range(NCH):
        near(1 + ch, v_grad, ch, core).start()
    big_forward(2)
    for ch in range(NCH):
        gather_mid.step(ch, 3)
        near(3 + ch, v_mid, ch, core).start()
    for ch in range(NCH):
        near(1 + ch, v_grad, ch, 1 - core).wait_recv()
        near(3 + ch, v_mid, ch, 1 - core).wait_recv()
    outs = [
        pltpu.make_async_copy(src, dst, out_sem.at[i])
        for i, (src, dst) in enumerate(
            (
                (v_proj, proj),
                (v_in, rows_in),
                (v_pair, pair),
                (v_mixed, mixed),
                (v_mid, rows_mid),
                (v_grad, rows_grad),
            )
        )
    ]
    for copy in outs:
        copy.start()
    for k in range(3):
        big_finish(k)
    for copy in proj_out:
        copy.wait_send()
    pair_out.wait_send()
    for ch in range(NCH):
        near(1 + ch, v_grad, ch, core).wait_send()
        near(3 + ch, v_mid, ch, core).wait_send()
    for line in (gather_in, gather_grad, gather_mid, scatter):
        line.drain()
    for copy in outs:
        copy.wait()


def allowed(core, ch, unit, depth, wide):
    def place_of(row):
        chunk, rest = row // wide, lax.rem(row, wide)
        return (rest // unit) * (unit * NCH) + chunk * unit + lax.rem(rest, unit)

    keys = NCH * wide
    query = lax.broadcasted_iota(jnp.int32, (wide, 2 * keys), 0)
    key = lax.broadcasted_iota(jnp.int32, (wide, 2 * keys), 1)
    key_at = (key // keys) * keys + place_of(lax.rem(key, keys))
    return key_at <= core * keys + place_of(query + ch * wide)


def both(pair, first):
    return pair[:, :, first : first + HD].reshape(-1, HD)


def softmax(queries, pair, keep):
    scores = dot(queries, both(pair, 0), 1, 1) * (1.0 / math.sqrt(HD))
    scores = jnp.where(keep, scores, NEG)
    weights = jnp.exp(scores - jnp.max(scores, -1, keepdims=True))
    probs = weights / jnp.sum(weights, -1, keepdims=True)
    return probs, probs.astype(BF16)


def forward_call(depth, args):
    rows, width = args[0].shape
    total_rows = rows * depth
    shard, q_width = args[4].shape
    d_model = width
    unit = rows // NCH
    vm = pl.BlockSpec(memory_space=pltpu.VMEM)
    anyspace = pl.BlockSpec(memory_space=pl.ANY)
    sds = jax.ShapeDtypeStruct
    dma = pltpu.SemaphoreType.DMA
    out_shape = (
        sds((3, d_model, HALF), BF16),
        sds((d_model, 2 * q_width + 2 * HD), BF16),
        sds((total_rows, width), BF16),
        sds((q_width // HD, total_rows, HD), BF16),
        sds((2, total_rows, 2 * HD), BF16),
        sds((total_rows, q_width), BF16),
        sds((rows, width), F32),
        sds((2, total_rows, width), BF16),
        sds((2, total_rows, width), BF16),
    )
    return pl.pallas_call(
        forward_kernel,
        out_shape=out_shape,
        in_specs=[vm] * len(args),
        out_specs=(anyspace, anyspace, anyspace, vm, anyspace, anyspace, vm, anyspace, anyspace),
        scratch_shapes=[
            pltpu.VMEM((3, shard, HALF), BF16),
            pltpu.VMEM((d_model, 2 * q_width + 2 * HD), BF16),
            pltpu.VMEM((total_rows, width), BF16),
            pltpu.VMEM((2, total_rows, 2 * HD), BF16),
            pltpu.VMEM((total_rows, q_width), BF16),
            pltpu.VMEM((2, total_rows, width), BF16),
            pltpu.VMEM((2, total_rows, width), BF16),
            pltpu.VMEM((total_rows, width), BF16),
            pltpu.VMEM((2, NCH, depth - 1, unit, width), BF16),
            pltpu.VMEM((unit, width), F32),
            dma((3, 4, 2)),
            dma((3, 4, 2)),
            dma((8,)),
            dma((8,)),
            dma((3,)),
            dma((3, 2, NCH, depth)),
            dma((3, 2, NCH, depth)),
            dma((2, NCH, depth)),
            dma((2, NCH, depth)),
            dma((1 + 2 * NCH,)),
            dma((1 + 2 * NCH,)),
            dma((6,)),
        ],
        compiler_params=pltpu.CompilerParams(
            collective_id=0, has_side_effects=True, vmem_limit_bytes=58 * 2**20
        ),
        cost_estimate=pl.CostEstimate(flops=4 * 10**9, bytes_accessed=3 * 10**7, transcendentals=0),
    )(*args)


class SquareScatter:
    def __init__(self, place, block, via, final, send, recv, stage=None):
        self.p, self.block, self.via, self.final = place, block, via, final
        self.send, self.recv, self.stage = send, recv, stage

    def _copy(self, i):
        p = self.p
        chip, half, way, row = (
            (p.dchip, 0, 0, 0),
            (p.dchip, 1, 1, 0),
            (p.xchip, 0, 0, 1),
            (p.ychip, 1, 1, 2),
            (p.xchip, 1, 0, 1),
            (p.ychip, 0, 1, 2),
        )[i]
        land = self.via.at[way] if row == 0 else self.final.at[way, half]
        return rcopy(
            self.block(chip, half),
            land,
            self.send.at[row, half],
            self.recv.at[row, half],
            (p.xnbr, p.ynbr)[way],
        )

    def start(self, *which):
        for i in which:
            self._copy(i).start()

    def second(self):
        p = self.p
        for way, chip, i in ((1, p.xchip, 4), (0, p.ychip, 5)):
            self._copy(way).wait_recv()
            block = self.block(chip, way)
            if self.stage is None:
                more = self.via[way]
            else:
                fetch = pltpu.make_async_copy(self.via.at[way], *self.stage)
                fetch.start()
                fetch.wait()
                more = self.stage[0][...]
            block[...] = (block[...].astype(F32) + more.astype(F32)).astype(BF16)
            self.start(i)

    def arrive(self, way, r):
        here = self.final.at[way, r]
        rcopy(
            here, here, self.send.at[1 + way, r], self.recv.at[1 + way, r], self.p.xnbr
        ).wait_recv()

    def drain(self):
        for i in range(6):
            self._copy(i).wait_send()


def norm_back(rows, grad, gain):
    root = inverse_root(rows)
    u = grad * gain
    back = root * u - rows * (root * root * root * jnp.mean(u * rows, -1, keepdims=True))
    return back, jnp.sum(grad * rows * root, 0, keepdims=True)


def backward_kernel(
    big, proj, rows_in, heads_q, pair, mixed, middle, rows_mid, rows_grad,
    tokens, grad_out, attn_gain, mlp_gain, cosine, sine,
    out, grad_in, g_gate, g_up, g_down, g_query, g_out, g_pair, sums, final, via, sib_land,
    vbig, hid, d_g, d_u, part, part_o, land, land_o, near_at, back, probs_at, d_s_at, d_mixed, d_lin, d_pair, pair_land,
    swap_land, d_middle, total, stage, result,
    gp, gp_land, gp_via_q, gp_fin_q, gp_via_o, gp_fin_o, pair_z, vec, vec_land,
    load_sem, s_send, s_recv, z_send, z_recv, near_send, near_recv, sq_send, sq_recv, sib_send, sib_recv,
    gp_send, gp_recv, misc_send, misc_recv, v_send, v_recv, stage_sem, out_sem, near_free,
):
    p = Place(4)
    z, core = p.z, p.core
    other = 1 - core
    unit = tokens.shape[0] // NCH
    wide = unit * p.depth
    d_model = tokens.shape[1]
    shard = d_model // 8
    q_width = mixed.shape[1]
    heads = q_width // HD
    scale = 1.0 / math.sqrt(HD)

    loads = [pltpu.make_async_copy(big.at[k], vbig.at[k], load_sem.at[k]) for k in range(3)]
    for copy in loads:
        copy.start()
    p.greet(False)
    for copy in loads:
        copy.wait()

    def rows_of(ref, ch, s):
        return ref.at[pl.ds(pl.multiple_of(ch * wide + s * unit, unit), unit), :]

    scatter_a = LineScatter(p, lambda ch, s: rows_of(part, ch, s), land, s_send.at[0], s_recv.at[0])
    scatter_o = LineScatter(
        p, lambda ch, s: rows_of(part_o, ch, s), land_o, s_send.at[1], s_recv.at[1]
    )
    scatter_i = LineScatter(p, lambda ch, s: rows_of(part, ch, s), land, s_send.at[2], s_recv.at[2])
    gather_back = LineGather(p, lambda ch, s: rows_of(back, ch, s), z_send, z_recv)

    def near(k, ch):
        return rcopy(
            near_at.at[0, ch], near_at.at[1, ch], near_send.at[k, ch], near_recv.at[k, ch], p.sib
        )

    def hidden(slot, ch):
        rows = pl.ds(ch * wide, wide)
        a2 = rows_mid[slot, rows, :]
        go = rows_grad[slot, rows, :]
        for first in range(0, HALF, 256):
            cols = slice(first, min(first + 256, HALF))
            gate = dot(a2, vbig[0, :, cols])
            up = dot(a2, vbig[1, :, cols])
            d_m = dot(go, vbig[2, :, cols])
            sg = 1.0 / (1.0 + jnp.exp(-gate))
            silu = gate * sg
            hid[slot, rows, cols] = (silu * up).astype(BF16)
            d_g[slot, rows, cols] = (d_m * up * sg * (1.0 + gate * (1.0 - sg))).astype(BF16)
            d_u[slot, rows, cols] = (d_m * silu).astype(BF16)

    def d_mid_rows(slot, ch):
        rows = pl.ds(ch * wide, wide)
        return dot(d_g[slot, rows, :], vbig[0], 1, 1) + dot(d_u[slot, rows, :], vbig[1], 1, 1)

    for ch in range(NCH):
        hidden(other, ch)
        near_at[0, ch] = d_mid_rows(other, ch).astype(BF16)
        near(0, ch).start()
    for ch in range(NCH):
        hidden(core, ch)
        term = d_mid_rows(core, ch)
        near(0, ch).wait_recv()
        part[ch * wide : (ch + 1) * wide, :] = (term + near_at[1, ch].astype(F32)).astype(BF16)
        scatter_a.step(ch, 3)
    pl.semaphore_signal(near_free, inc=1, device_id=p.sib, device_id_type=MESH)

    for ch in range(NCH):
        rows = pl.ds(ch * wide, wide)
        near(0, ch).wait_send()
        near_at[0, ch] = dot(hid[other, rows, :], vbig[2], 1, 1).astype(BF16)
        if ch == 0:
            pl.semaphore_wait(near_free, 1)
        near(1, ch).start()
    for ch in range(NCH):
        scatter_a.step(ch, 2)
    for ch in range(NCH):
        rows = pl.ds(ch * wide, wide)
        term = dot(hid[core, rows, :], vbig[2], 1, 1)
        near(1, ch).wait_recv()
        part_o[ch * wide : (ch + 1) * wide, :] = (term + near_at[1, ch].astype(F32)).astype(BF16)
    for ch in range(NCH):
        scatter_a.step(ch, 1)

    squares = [
        SquareScatter(
            p,
            lambda chip, r, k=k: vbig.at[
                k, pl.ds(pl.multiple_of((chip * 2 + r) * shard, 16), shard), :
            ],
            via.at[k],
            final.at[k],
            sq_send.at[k],
            sq_recv.at[k],
            (stage.at[0], stage_sem.at[0]),
        )
        for k in range(3)
    ]

    def weight_grad(k, chip):
        wide_cols = pl.ds(pl.multiple_of(chip * 2 * shard, HD), 2 * shard)
        left = rows_grad if k == 2 else rows_mid
        right = (d_g, d_u, hid)[k]
        term = dot(left[0, :, wide_cols], right[0], 0, 0) + dot(left[1, :, wide_cols], right[1], 0, 0)
        vbig[k, pl.ds(pl.multiple_of(chip * 2 * shard, 16), 2 * shard), :] = term.astype(BF16)

    def weight_grads(k):
        weight_grad(k, p.dchip)
        squares[k].start(0, 1)
        weight_grad(k, p.xchip)
        squares[k].start(2)
        weight_grad(k, p.ychip)
        squares[k].start(3)
        weight_grad(k, p.chip)

    weight_grads(0)
    gain_sum = jnp.zeros((1, d_model), F32)
    for ch in range(NCH):
        half = slice(ch * unit, (ch + 1) * unit)
        scatter_a.total(ch, total)
        grad, gain_part = norm_back(middle[half, :], total[...], mlp_gain[...])
        gain_sum = gain_sum + gain_part
        d_mid = grad_out[half, :].astype(F32) + grad
        d_middle[half, :] = d_mid
        back[pl.ds(pl.multiple_of(ch * wide + z * unit, unit), unit), :] = d_mid.astype(BF16)
        gather_back.own(ch)
    scatter_a.drain()
    for ch in range(NCH):
        scatter_o.step(ch, 3)
    weight_grads(1)
    for ch in range(NCH):
        gather_back.step(ch, 1)
        scatter_o.step(ch, 2)
    weight_grads(2)
    squares[0].second()
    for ch in range(NCH):
        gather_back.step(ch, 2)
        scatter_o.step(ch, 1)
    squares[1].second()
    for ch in range(NCH):
        gather_back.step(ch, 3)

    fetch_in = [
        pltpu.make_async_copy(
            rows_in.at[pl.ds(ch * wide, wide), :], near_at.at[0, ch], load_sem.at[3 + ch]
        )
        for ch in range(NCH)
    ]
    for ch in range(NCH):
        near(1, ch).wait_send()
        fetch_in[ch].start()
    d_pair[...] = jnp.zeros(d_pair.shape, F32)
    for ch in range(NCH):
        rows = pl.ds(ch * wide, wide)
        d_mixed[rows, :] = dot(back[rows, :], proj[:, q_width + 2 * HD :]).astype(BF16)

        def one_head(h):
            cols = slice(h * HD, (h + 1) * HD)
            keep = allowed(core, ch, unit, p.depth, wide)
            queries = heads_q[h, rows, :]
            probs, pb = softmax(queries, pair, keep)
            d_o = d_mixed[rows, cols]
            d_p = dot(d_o, both(pair, HD), 1, 1)
            d_s_at[...] = (probs * (d_p - jnp.sum(probs * d_p, -1, keepdims=True))).astype(BF16)
            probs_at[...] = pb
            keys = NCH * wide
            d_q = dot(d_s_at[...], both(pair, 0)) * scale
            d_lin[rows, cols] = turn(d_q, cosine[rows, :], -sine[rows, :]).astype(BF16)
            for slot in (0, 1):
                span = slice(slot * keys, (slot + 1) * keys)
                d_pair[slot, :, 0:HD] += dot(d_s_at[:, span], queries, 0, 0) * scale
                d_pair[slot, :, HD:] += dot(probs_at[:, span], d_o, 0, 0)

        for h in range(heads):
            one_head(h)

    pair_land[0] = d_pair[other].astype(BF16)
    across = rcopy(
        pair_land.at[0], pair_land.at[1], misc_send.at[0], misc_recv.at[0], p.sib
    )
    across.start()
    gp_out = q_width + HD
    for chip in range(4):
        wide_cols = slice(chip * 2 * shard, (chip + 1) * 2 * shard)
        gp[wide_cols, gp_out:] = dot(back[:, wide_cols], mixed[...], 0, 0).astype(BF16)
    across.wait_recv()
    d_pair[core] += pair_land[1].astype(F32)
    which = lax.rem(z, 2)
    mine = pl.ds(pl.multiple_of(which * HD, HD), HD)
    theirs = pl.ds(pl.multiple_of((1 - which) * HD, HD), HD)
    swap_land[0] = d_pair[core, :, theirs].astype(BF16)
    swap = rcopy(
        swap_land.at[0],
        swap_land.at[1],
        misc_send.at[1],
        misc_recv.at[1],
        (p.dp, z + 1 - 2 * which),
    )
    swap.start()
    squares[2].second()
    swap.wait_recv()
    own = d_pair[core, :, mine] + swap_land[1].astype(F32)
    is_key = which == 0
    own = own * jnp.where(is_key, cosine[...], 1.0) - pltpu.roll(own, HD // 2, 1) * jnp.where(
        is_key, sine[...], 0.0
    )
    d_lin[:, q_width:] = own.astype(BF16)

    w_mine = proj[:, pl.ds(pl.multiple_of(q_width + which * HD, HD), HD)]
    for ch in range(NCH):
        rows = slice(ch * wide, (ch + 1) * wide)
        part[rows, :] = (
            dot(d_lin[rows, :q_width], proj[:, :q_width], 1, 1) + dot(d_lin[rows, q_width:], w_mine, 1, 1)
        ).astype(BF16)
        scatter_i.step(ch, 3)
    for copy in fetch_in:
        copy.wait()
    for chip in range(4):
        wide_cols = slice(chip * 2 * shard, (chip + 1) * 2 * shard)
        gp[wide_cols, :gp_out] = (
            dot(near_at[0, 0, :, wide_cols], d_lin[:wide, :], 0, 0)
            + dot(near_at[0, 1, :, wide_cols], d_lin[wide:, :], 0, 0)
        ).astype(BF16)

    def gp_near(chip):
        src = gp.at[pl.ds(pl.multiple_of((chip * 2 + other) * shard, 16), shard), :]
        return rcopy(src, gp_land.at[chip], misc_send.at[2 + chip], misc_recv.at[2 + chip], p.sib)

    for chip in range(4):
        gp_near(chip).start()
    for ch in range(NCH):
        scatter_i.step(ch, 2)

    def gp_rows(chip):
        return pl.ds(pl.multiple_of((chip * 2 + core) * shard, 16), shard)

    for chip in range(4):
        gp_near(chip).wait_recv()
        gp[gp_rows(chip), :] = (
            gp[gp_rows(chip), :].astype(F32) + gp_land[chip].astype(F32)
        ).astype(BF16)
    half_rows = shard // 2
    gp_squares = [
        SquareScatter(
            p,
            lambda chip, r, cols=cols: gp.at[
                pl.ds(pl.multiple_of((chip * 2 + core) * shard + r * half_rows, 16), half_rows),
                cols,
            ],
            gvia,
            gfin,
            gp_send.at[i],
            gp_recv.at[i],
        )
        for i, (cols, gvia, gfin) in enumerate(
            ((slice(0, gp_out), gp_via_q, gp_fin_q), (slice(gp_out, gp_out + q_width), gp_via_o, gp_fin_o))
        )
    ]
    for square in gp_squares:
        square.start(0, 1, 2, 3)
    for ch in range(NCH):
        scatter_i.step(ch, 1)
    for ch in range(NCH):
        half = slice(ch * unit, (ch + 1) * unit)
        scatter_o.total(ch, total)
        out[half, :] = middle[half, :] + total[...]
    for square in gp_squares:
        square.second()

    def kept(k, r):
        for way in (0, 1):
            squares[k].arrive(way, r)
        fetch = [
            pltpu.make_async_copy(final.at[k, way, r], stage.at[way], stage_sem.at[way])
            for way in (0, 1)
        ]
        for copy in fetch:
            copy.start()
        for copy in fetch:
            copy.wait()
        block = big_block(k, r)[...]
        return block.astype(F32) + stage[0].astype(F32) + stage[1].astype(F32)

    def big_block(k, r):
        return vbig.at[k, pl.ds(pl.multiple_of((p.chip * 2 + r) * shard, 16), shard), :]

    def sib_copy(k):
        return rcopy(big_block(k, other), sib_land.at[k], sib_send.at[k], sib_recv.at[k], p.sib)

    def keep_big(k):
        big_block(k, other)[...] = kept(k, other).astype(BF16)
        sib_copy(k).start()

    def result_copy(k):
        return pltpu.make_async_copy(result, (g_gate, g_up, g_down)[k], out_sem.at[k])

    def finish_big(k):
        own = kept(k, core)
        sib_copy(k).wait_recv()
        fetch = pltpu.make_async_copy(sib_land.at[k], stage.at[0], stage_sem.at[0])
        fetch.start()
        fetch.wait()
        if k > 0:
            result_copy(k - 1).wait()
        theirs = stage[0].astype(F32)
        cols = result.shape[1]
        for c in (0, 1):

            @pl.when(core == c)
            def _(c=c):
                result[:, :HALF] = own if c == 0 else theirs
                result[:, HALF:] = (theirs if c == 0 else own)[:, : cols - HALF]

        result_copy(k).start()

    keep_big(0)
    in_gain = jnp.zeros((1, d_model), F32)
    for ch in range(NCH):
        half = slice(ch * unit, (ch + 1) * unit)
        scatter_i.total(ch, total)
        grad, gain_part = norm_back(tokens[half, :].astype(F32), total[...], attn_gain[...])
        in_gain = in_gain + gain_part
        grad_in[half, :] = d_middle[half, :] + grad

    vec[...] = jnp.zeros(vec.shape, F32)
    bias = jnp.sum(d_lin[...].astype(F32), 0, keepdims=True)
    for i in range(heads):
        vec[pl.ds(z * heads + i, 1), :] = bias[:, i * HD : (i + 1) * HD]
    n_q = heads * p.depth
    vec[pl.ds(n_q + which * 2 + z // 2, 1), :] = bias[:, q_width:]
    for i in range(d_model // HD):
        cols = slice(i * HD, (i + 1) * HD)
        vec[n_q + 4 + i : n_q + 5 + i, :] = in_gain[:, cols]
        vec[n_q + 4 + d_model // HD + i : n_q + 5 + d_model // HD + i, :] = gain_sum[:, cols]
    for i, dev in enumerate((p.sib, p.xnbr, p.ynbr)):
        step = rcopy(vec, vec_land.at[i], v_send.at[i], v_recv.at[i], dev)
        step.start()
        step.wait()
        vec[...] += vec_land[i]

    def z_other(d):
        return lax.rem(z + d, p.depth)

    keep_big(1)
    keep_big(2)
    for i, square in enumerate(gp_squares):
        for r in (0, 1):
            square.arrive(0, r)
            square.arrive(1, r)
            cols, fin = ((slice(0, gp_out), gp_fin_q), (slice(gp_out, gp_out + q_width), gp_fin_o))[i]
            block = gp[
                pl.ds(pl.multiple_of((p.chip * 2 + core) * shard + r * half_rows, 16), half_rows), cols
            ]
            value = block.astype(F32) + fin[0, r].astype(F32) + fin[1, r].astype(F32)
            rows = slice(r * half_rows, (r + 1) * half_rows)
            if i == 0:
                g_query[rows, :] = value[:, :q_width]
                pair_z[0, rows, :] = value[:, q_width:]
            else:
                g_out[rows, :] = value

    quarter = shard // p.depth
    g_pair[z] = pair_z[0, pl.ds(pl.multiple_of(z * quarter, 8), quarter), :]

    def along(d):
        dev = (p.dp, z_other(d))
        return (
            rcopy(
                pair_z.at[0, pl.ds(pl.multiple_of(z_other(d) * quarter, 8), quarter), :],
                pair_z.at[1, pl.ds((d - 1) * quarter, quarter), :],
                v_send.at[2 + d],
                v_recv.at[2 + d],
                dev,
            ),
            rcopy(vec, vec_land.at[2 + d], v_send.at[5 + d], v_recv.at[5 + d], dev),
        )

    for d in (1, 2, 3):
        for copy in along(d):
            copy.start()
    for k in range(3):
        finish_big(k)
    for d in (1, 2, 3):
        for copy in along(d):
            copy.wait()
        g_pair[lax.rem(z + p.depth - d, p.depth)] = pair_z[1, (d - 1) * quarter : d * quarter, :]
    sums[...] = vec[...] + vec_land[3] + vec_land[4] + vec_land[5]

    for line in (scatter_o, scatter_i, gather_back):
        line.drain()
    for square in squares + gp_squares:
        square.drain()
    across.wait_send()
    swap.wait_send()
    for chip in range(4):
        gp_near(chip).wait_send()
    for k in range(3):
        sib_copy(k).wait_send()
    result_copy(2).wait()


def backward_call(depth, args, cols):
    big, proj, rows_in, heads_q, pair, mixed, middle = args[:7]
    rows, d_model = middle.shape
    q_width = mixed.shape[1]
    total_rows = rows * depth
    unit = rows // NCH
    wide = unit * depth
    shard = d_model // 8
    vm = pl.BlockSpec(memory_space=pltpu.VMEM)
    anyspace = pl.BlockSpec(memory_space=pl.ANY)
    sds = jax.ShapeDtypeStruct
    dma = pltpu.SemaphoreType.DMA
    n_sum = 2 * d_model // HD + d_model // HD + 4
    n_sum = -(-n_sum // 8) * 8
    gp_cols = q_width + HD + q_width
    half_rows = shard // 2
    out_shape = (
        sds((rows, d_model), F32),
        sds((rows, d_model), F32),
        sds((shard, cols), F32),
        sds((shard, cols), F32),
        sds((shard, cols), F32),
        sds((shard, q_width), F32),
        sds((shard, q_width), F32),
        sds((depth, shard // depth, HD), F32),
        sds((n_sum, HD), F32),
        sds((3, 2, 2, shard, HALF), BF16),
        sds((3, 2, shard, HALF), BF16),
        sds((3, shard, HALF), BF16),
    )
    v = pltpu.VMEM
    return pl.pallas_call(
        backward_kernel,
        out_shape=out_shape,
        in_specs=[anyspace, vm, anyspace] + [vm] * (len(args) - 3),
        out_specs=(vm, vm, anyspace, anyspace, anyspace, vm, vm, vm, vm, anyspace, anyspace, anyspace),
        scratch_shapes=[
            v((3, d_model, HALF), BF16),
            v((2, total_rows, HALF), BF16),
            v((2, total_rows, HALF), BF16),
            v((2, total_rows, HALF), BF16),
            v((total_rows, d_model), BF16),
            v((total_rows, d_model), BF16),
            v((2, NCH, depth - 1, unit, d_model), BF16),
            v((2, NCH, depth - 1, unit, d_model), BF16),
            v((2, NCH, wide, d_model), BF16),
            v((total_rows, d_model), BF16),
            v((wide, 2 * total_rows), BF16),
            v((wide, 2 * total_rows), BF16),
            v((total_rows, q_width), BF16),
            v((total_rows, q_width + HD), BF16),
            v((2, total_rows, 2 * HD), F32),
            v((2, total_rows, 2 * HD), BF16),
            v((2, total_rows, HD), BF16),
            v((rows, d_model), F32),
            v((unit, d_model), F32),
            v((2, shard, HALF), BF16),
            v((shard, cols), F32),
            v((d_model, gp_cols), BF16),
            v((4, shard, gp_cols), BF16),
            v((2, half_rows, q_width + HD), BF16),
            v((2, 2, half_rows, q_width + HD), BF16),
            v((2, half_rows, q_width), BF16),
            v((2, 2, half_rows, q_width), BF16),
            v((2, shard, HD), F32),
            v((n_sum, HD), F32),
            v((6, n_sum, HD), F32),
            dma((3 + NCH,)),
            dma((3, 2, NCH, depth)),
            dma((3, 2, NCH, depth)),
            dma((2, NCH, depth)),
            dma((2, NCH, depth)),
            dma((2, NCH)),
            dma((2, NCH)),
            dma((3, 3, 2)),
            dma((3, 3, 2)),
            dma((3,)),
            dma((3,)),
            dma((2, 3, 2)),
            dma((2, 3, 2)),
            dma((6,)),
            dma((6,)),
            dma((9,)),
            dma((9,)),
            dma((2,)),
            dma((3,)),
            pltpu.SemaphoreType.REGULAR,
        ],
        compiler_params=pltpu.CompilerParams(
            collective_id=1, has_side_effects=True, vmem_limit_bytes=62 * 2**20
        ),
        cost_estimate=pl.CostEstimate(flops=4 * 10**10, bytes_accessed=5 * 10**7, transcendentals=0),
    )(*args)


def chunk_order(rows, depth):
    unit = rows.shape[0] // (depth * NCH)
    return rows.reshape(depth, NCH, unit, *rows.shape[1:]).swapaxes(0, 1).reshape(rows.shape)


def paired_shards(
    tokens, grad_out, attn_gain, w_query, b_query, w_key, b_key, w_value, b_value, w_out, mlp_gain, w_gate, w_up, w_down
):
    depth = lax.axis_size("tensor")
    rows = tokens.shape[0] * depth
    members = lax.axis_size("dp") // GROUPS
    group_tok = members * rows
    position, _ = layout(lax.axis_index("dp") * rows, rows, group_tok, group_tok // 2)
    cosine, sine = tables(chunk_order(position, depth), HD)
    half = HD // 2
    sine = jnp.concatenate([-sine[:, :half], sine[:, half:]], 1)
    gains = (attn_gain[None], mlp_gain[None])
    biases = (b_query[None], b_key[None], b_value[None])
    kept = forward_call(
        depth,
        (tokens, grad_out, *gains, w_query, w_key, w_value, w_out, w_gate, w_up, w_down, *biases, cosine, sine),
    )
    got = backward_call(depth, (*kept, tokens, grad_out, *gains, cosine, sine), w_gate.shape[1])
    out, grad_in, g_gate, g_up, g_down, g_query, g_out, g_pair, sums = got[:9]
    flat = sums.reshape(-1)
    place = lax.axis_index("dp") * depth + lax.axis_index("tensor")
    count = lax.axis_size("dp") * depth
    parts, first = [], 0
    for size in (b_query.shape[0], b_key.shape[0], b_value.shape[0], attn_gain.shape[0], mlp_gain.shape[0]):
        parts.append(lax.dynamic_slice_in_dim(flat, first + place * (size // count), size // count))
        first += size
    g_key = jnp.concatenate([g_pair[0], g_pair[2]], 1)
    g_value = jnp.concatenate([g_pair[1], g_pair[3]], 1)
    return (
        out, grad_in, parts[3], g_query, parts[0], g_key, parts[1], g_value, parts[2], g_out, parts[4], g_gate, g_up, g_down
    )


def solution(mesh):
    paired = mesh.shape["dp"] == 2 * GROUPS and mesh.shape["tensor"] == 4
    return jax.shard_map(
        paired_shards if paired else shards,
        mesh=mesh,
        in_specs=(
            P(("dp", "tensor"), None),
            P(("dp", "tensor"), None),
            P(),
            P("dp", "tensor"),
            P(),
            P("dp", None),
            P(),
            P("dp", None),
            P(),
            P("dp", "tensor"),
            P(),
            P("dp", "tensor"),
            P("dp", "tensor"),
            P("dp", "tensor"),
        ),
        out_specs=(
            P(("dp", "tensor"), None),
            P(("dp", "tensor"), None),
            P(("dp", "tensor")),
            P("dp", "tensor"),
            P(("dp", "tensor")),
            P(("dp", "tensor"), None),
            P(("dp", "tensor")),
            P(("dp", "tensor"), None),
            P(("dp", "tensor")),
            P("dp", "tensor"),
            P(("dp", "tensor")),
            P("dp", "tensor"),
            P("dp", "tensor"),
            P("dp", "tensor"),
        ),
        check_vma=False,
    )
```
